256 devices in a mesh: dp: 64 (over y, z, core), tensor: 4 (over x).
Axes of the slice: x: 4, y: 4, z: 8, core: 2. Of those that a mesh axis runs over, the one named last changes fastest.
Arguments:
- patches: bfloat16 [32768, 1280], P('dp', 'tensor'), may hold values from -64 to 64
- counts: int32 [512], replicated, may hold values from 32 to 64, as said below
- source_slot: int32 [512], replicated, may hold values from 0 to 511, as said below
- target_slot: int32 [512], replicated, may hold values from 0 to 511, as said below
- lang_start: int32 [512], replicated, may hold values from 0 to 10232, as said below
- window_order: int32 [512, 16], replicated, may hold values from 0 to 15, as said below
- norm_gain: float32 [1280], replicated, may hold values from 0.1 to 1.9
- qkv_weight: bfloat16 [1280, 3, 1280], P(None, None, 'tensor'), may hold values from -1 to 1
- qkv_bias: float32 [3, 1280], P(None, 'tensor'), may hold values from -3 to 3
- proj_weight: bfloat16 [1280, 1280], P('tensor'), may hold values from -0.15625 to 0.15625
- proj_bias: float32 [1280], replicated, may hold values from -3 to 3
- merge_gain: float32 [1280], replicated, may hold values from 0.1 to 1.9
- expand_weight: bfloat16 [5120, 2560], P('dp', 'tensor'), may hold values from -0.078125 to 0.078125
- expand_bias: float32 [2560], P('tensor'), may hold values from -3 to 3
- output_weight: bfloat16 [2560, 4096], P('tensor', 'dp'), may hold values from -0.125 to 0.125
- output_bias: float32 [4096], P('tensor'), may hold values from -3 to 3
Outputs:
- encoded: bfloat16 [32768, 1280], P('dp', 'tensor')
- merged: bfloat16 [10240, 4096], P('dp', 'tensor')
The draws below stay inside these ranges and needn't reach their ends.
Inputs may be any that keep to these rules, and one draw needn't show every extreme that they name: `counts`: each count is a multiple of 4. `source_slot`: A permutation of the 512 slots; slot s lies on data rank s // 8. `target_slot`: A permutation of the slots; at most 1 images go from one source rank to one target rank. `lang_start`: image i's merged rows lie inside the shard of rank i // 8 (160 rows each), in increasing order of i without intersection; at most 1 images go from one target rank to one shard. `window_order`: for image i the first counts[i] / 4 entries are a permutation of 0 to counts[i] / 4 - 1; entry j beyond them is j.
All inputs are finite; a program needn't handle non-finite values.
Results may differ from the reference program's by a relative error of at most 0.019.
Values may be sent and summed in bfloat16 or wider, within the bound.
No kernel may reach another device: no remote copies, remote signals or barrier semaphores. Data moves between devices by JAX's collectives and lax.ppermute only.
A program may use at most 64 MiB of HBM per device.

```python
import math
import jax
import jax.numpy as jnp
from jax import lax

D = 1280
HEADS = 16
HD = 80
MH = 2560
MO = 4096
CAP = 64
IMG_DEV = 8
MCAP = 16
NIMG = 512
LROWS = 160
N_DP = 64
N_TENSOR = 4


def layout(key):
    key_list = jax.random.split(key, 11)
    image_total = IMG_DEV * N_DP
    image_ids = jnp.arange(image_total, dtype=jnp.int32)
    lang_rank = image_ids // IMG_DEV
    column = image_ids % IMG_DEV
    first_mix = jax.random.permutation(key_list[0], N_DP)
    first_shift = jax.random.permutation(key_list[1], N_DP)
    second_mix = jax.random.permutation(key_list[2], N_DP)
    second_shift = jax.random.permutation(key_list[3], N_DP)
    target_rank = first_mix[(first_shift[lang_rank] + column) % N_DP]
    source_rank = second_mix[(second_shift[target_rank] + column) % N_DP]
    target_order = jax.vmap(lambda sub_key: jax.random.permutation(sub_key, IMG_DEV))(jax.random.split(key_list[4], N_DP))
    source_order = jax.vmap(lambda sub_key: jax.random.permutation(sub_key, IMG_DEV))(jax.random.split(key_list[5], N_DP))
    target_slot = (target_rank * IMG_DEV + target_order[target_rank, column]).astype(jnp.int32)
    source_slot = (source_rank * IMG_DEV + source_order[source_rank, column]).astype(jnp.int32)
    floor_q = jax.random.randint(key_list[6], (N_DP,), CAP // 8, CAP // 4 + 1)
    raw_draws = jax.random.randint(key_list[7], (image_total,), 0, 1 << 20)
    span_size = CAP // 4 + 1 - floor_q[source_rank]
    quarter = floor_q[source_rank] + raw_draws % span_size
    chosen = jax.random.randint(key_list[8], (), 0, image_total)
    quarter = jnp.where(image_ids == chosen, CAP // 4, quarter)
    counts = (4 * quarter).astype(jnp.int32)
    segment = MCAP + MCAP // 4
    slack_rows = segment - quarter + 1
    gap_rows = jax.random.randint(key_list[9], (image_total,), 0, 1 << 20) % slack_rows
    lang_start = (lang_rank * LROWS + column * segment + gap_rows).astype(jnp.int32)
    noise_keys = jax.random.randint(key_list[10], (image_total, MCAP), 0, 1 << 20)
    step_ids = jnp.arange(MCAP, dtype=jnp.int32)
    sort_keys = jnp.where(step_ids[None, :] < quarter[:, None], noise_keys * MCAP + step_ids[None, :], (1 << 26) + step_ids[None, :])
    order_rows = jnp.argsort(sort_keys, axis=1, stable=True).astype(jnp.int32)
    return (counts, source_slot, target_slot, lang_start, order_rows)


def draw_counts(key, part):
    shared = layout(key)
    return shared[0]


def draw_source_slot(key, part):
    shared = layout(key)
    return shared[1]


def draw_target_slot(key, part):
    shared = layout(key)
    return shared[2]


def draw_lang_start(key, part):
    shared = layout(key)
    return shared[3]


def draw_window_order(key, part):
    shared = layout(key)
    return shared[4]


def draw_patches(key, part):
    key = jax.random.fold_in(key, 21)
    key_parts = jax.random.split(key, 1)
    full_shape = (N_DP * IMG_DEV * CAP, D)
    values = jax.random.normal(key_parts[0], full_shape, jnp.float32)
    return jnp.clip(values, -8.0, 8.0).astype(jnp.bfloat16)


def draw_qkv_weight(key, part):
    key = jax.random.fold_in(key, 31)
    key_parts = jax.random.split(key, 1)
    base_draw = jnp.clip(jax.random.normal(key_parts[0], (D, 3, D), jnp.float32), -6.0, 6.0) / math.sqrt(D)
    return base_draw.astype(jnp.bfloat16)


def shard_levels(key, dims, cuts, smallest, top_value):
    level, own = 1.0, jax.random.fold_in(key, 6)
    for axis_at, blocks in cuts:
        heights = jnp.exp(jax.random.uniform(jax.random.fold_in(own, axis_at), (blocks,), jnp.float32, smallest / len(cuts), top_value / len(cuts)))
        level = level * jnp.repeat(heights, dims[axis_at] // blocks).reshape([-1 if axis == axis_at else 1 for axis in range(len(dims))])
    return level


def gaussian(own_key, shape, deviation, limit, cuts=(), held_as=jnp.bfloat16):
    values = deviation * jax.random.normal(own_key, shape, jnp.float32)
    if cuts:
        values = values * shard_levels(own_key, shape, cuts, -0.22, 0.18)
    return jnp.clip(values, -limit, limit).astype(held_as)


def setup_inputs(seed: int = 0) -> dict:
    key_of = jax.random.split(jax.random.key(seed), 17)
    return {
        "patches": draw_patches(jax.random.fold_in(key_of[16], 71), 0),
        "counts": draw_counts(jax.random.fold_in(key_of[16], 71), 0),
        "source_slot": draw_source_slot(jax.random.fold_in(key_of[16], 71), 0),
        "target_slot": draw_target_slot(jax.random.fold_in(key_of[16], 71), 0),
        "lang_start": draw_lang_start(jax.random.fold_in(key_of[16], 71), 0),
        "window_order": draw_window_order(jax.random.fold_in(key_of[16], 71), 0),
        "norm_gain": jnp.clip(1.0 + 0.18 * jax.random.normal(key_of[6], (D,), jnp.float32), 0.1, 1.9),
        "qkv_weight": draw_qkv_weight(jax.random.fold_in(key_of[16], 71), 0),
        "qkv_bias": gaussian(key_of[8], (3, D), 0.5, 3.0, ((1, 4),), jnp.float32),
        "proj_weight": gaussian(key_of[9], (D, D), D ** -0.5, 0.15625, ((0, 4),)),
        "proj_bias": gaussian(key_of[10], (D,), 0.5, 3.0, (), jnp.float32),
        "merge_gain": jnp.clip(1.0 + 0.18 * jax.random.normal(key_of[11], (D,), jnp.float32), 0.1, 1.9),
        "expand_weight": gaussian(key_of[12], (4 * D, MH), (4 * D) ** -0.5, 0.078125, ((0, 64), (1, 4))),
        "expand_bias": gaussian(key_of[13], (MH,), 0.5, 3.0, ((0, 4),), jnp.float32),
        "output_weight": gaussian(key_of[14], (MH, MO), MH ** -0.5, 0.125, ((0, 4), (1, 64))),
        "output_bias": gaussian(key_of[15], (MO,), 0.5, 3.0, ((0, 4),), jnp.float32),
    }


EPSILON = 1e-06

def rms_rows(values, row_gain):
    values = values.astype(jnp.float32)
    mean_square = lax.optimization_barrier(jnp.mean(values * values, axis=-1, keepdims=True))
    return values * lax.rsqrt(mean_square + EPSILON) * row_gain.astype(jnp.float32)

def settle(values):
    return lax.optimization_barrier(values.astype(jnp.bfloat16)).astype(jnp.float32)

def reference(patches, counts, source_slot, target_slot, lang_start, window_order, norm_gain, qkv_weight, qkv_bias, proj_weight, proj_bias, merge_gain, expand_weight, expand_bias, output_weight, output_bias):
    slots_in = patches.reshape(NIMG, CAP, D)
    w_qkv = qkv_weight.astype(jnp.float32).reshape(D, 3 * D)
    b_qkv = qkv_bias.astype(jnp.float32).reshape(3 * D)
    w_proj = proj_weight.astype(jnp.float32).reshape(N_TENSOR, D // N_TENSOR, D)
    w_expand = expand_weight.astype(jnp.float32)
    w_output = output_weight.astype(jnp.float32).reshape(N_TENSOR, MH // N_TENSOR, MO)
    score_scale = 1.0 / math.sqrt(HD)
    row_ids = jnp.arange(CAP, dtype=jnp.int32)
    merged_ids = jnp.arange(MCAP, dtype=jnp.int32)

    def group_step(lang_rank):
        images = lang_rank * IMG_DEV + jnp.arange(IMG_DEV, dtype=jnp.int32)
        image_rows = jnp.take(slots_in, source_slot[images], axis=0)
        live_count = counts[images]
        live_rows = row_ids[None, :] < live_count[:, None]
        normed = settle(rms_rows(image_rows, norm_gain))
        qkv_rows = jnp.einsum('bcd,de->bce', normed, w_qkv) + b_qkv
        qkv_rows = settle(qkv_rows).reshape(IMG_DEV, CAP, 3, HEADS, HD)
        scores = jnp.einsum('bqhe,bkhe->bhqk', qkv_rows[:, :, 0], qkv_rows[:, :, 1]) * score_scale
        scores = jnp.where(live_rows[:, None, None, :], scores, -1e+30)
        weights = settle(jax.nn.softmax(scores, axis=-1))
        context = jnp.einsum('bhqk,bkhe->bqhe', weights, qkv_rows[:, :, 2])
        context = settle(context).reshape(IMG_DEV, CAP, N_TENSOR, D // N_TENSOR)
        head_parts = settle(jnp.einsum('bcgf,gfd->bcgd', context, w_proj))
        hidden = image_rows.astype(jnp.float32) + lax.optimization_barrier(jnp.sum(head_parts, axis=2)) + proj_bias.astype(jnp.float32)
        encoded = jnp.where(live_rows[:, :, None], hidden, 0.0).astype(jnp.bfloat16)
        merge_in = settle(rms_rows(encoded, merge_gain)).reshape(IMG_DEV, MCAP, 4 * D)
        expanded = jnp.einsum('bmk,kh->bmh', merge_in, w_expand) + expand_bias.astype(jnp.float32)
        expanded = settle(jax.nn.gelu(expanded, approximate=False)).reshape(IMG_DEV, MCAP, N_TENSOR, MH // N_TENSOR)
        out_parts = settle(jnp.einsum('bmgh,gho->bmgo', expanded, w_output))
        merged_rows = (lax.optimization_barrier(jnp.sum(out_parts, axis=2)) + output_bias.astype(jnp.float32)).astype(jnp.bfloat16)
        placed = jax.vmap(lambda rows_of, order_of: jnp.take(rows_of, order_of, axis=0))(merged_rows, window_order[images])
        first_row = lang_start[images] - lang_rank * LROWS
        used_rows = counts[images] // 4
        target = jnp.where(merged_ids[None, :] < used_rows[:, None], first_row[:, None] + merged_ids[None, :], LROWS)
        lang_shard = jnp.zeros((LROWS, MO), jnp.bfloat16).at[target.reshape(-1)].set(placed.reshape(IMG_DEV * MCAP, MO), mode='drop')
        return (encoded, lang_shard)
    encoded_all, shards = lax.map(group_step, jnp.arange(N_DP, dtype=jnp.int32))
    encoded_slots = jnp.zeros((NIMG, CAP, D), jnp.bfloat16).at[target_slot].set(encoded_all.reshape(NIMG, CAP, D))
    return (encoded_slots.reshape(NIMG * CAP, D), shards.reshape(N_DP * LROWS, MO))
```

```python
import functools
import math

import jax
import jax.numpy as jnp
from jax import lax
from jax.experimental import pallas as pl
from jax.experimental.pallas import tpu as pltpu
from jax.sharding import PartitionSpec as P

HD = 80
CAP = 64
LROWS = 160
NY, NZ, NC = 4, 8, 2
EPSILON = 1e-06
BF = jnp.bfloat16
F32 = jnp.float32
VMEM_BYTES = 40 * 1024 * 1024


def dot_tn(lhs, rhs):
    return lax.dot_general(lhs, rhs, (((0,), (0,)), ((), ())), preferred_element_type=F32)


def dot_nt(lhs, rhs):
    return lax.dot_general(lhs, rhs, (((1,), (1,)), ((), ())), preferred_element_type=F32)


def dot_nn(lhs, rhs):
    return jnp.dot(lhs, rhs, preferred_element_type=F32)


def params(**extra):
    return pltpu.CompilerParams(vmem_limit_bytes=VMEM_BYTES, **extra)


def whole(shape):
    return pl.BlockSpec(shape, lambda *_: (0,) * len(shape))


def attention_kernel(
    member_ref, a0, a1, a2, a3, gain, w_qkv, b_qkv, w_proj, key_tag, p0, p1, p2, p3, normed, context
):
    width, rows = normed.shape
    cols = width // 4
    heads = cols // HD
    member = member_ref[0]
    pieces = [ref[...].astype(F32) for ref in (a0, a1, a2, a3)]
    square = sum(jnp.sum(piece * piece, axis=0, keepdims=True) for piece in pieces)
    inverse = lax.rsqrt(square * (1.0 / width) + EPSILON)
    for shift, piece in enumerate(pieces):
        owner = lax.rem(member - shift + 4, 4)
        span = pl.ds(pl.multiple_of(owner * cols, 64), cols)
        normed[span, :] = (piece * inverse * gain[span, :]).astype(BF)
    qkv = (dot_nn(w_qkv[...], normed[...]) + b_qkv[...]).astype(BF)
    query_image = lax.broadcasted_iota(jnp.int32, (rows, rows), 1) // CAP + pl.program_id(0) * (
        rows // CAP
    )
    allowed = key_tag[...] == query_image
    for head in range(heads):
        query = qkv[head * HD : (head + 1) * HD]
        key = qkv[cols + head * HD : cols + (head + 1) * HD]
        value = qkv[2 * cols + head * HD : 2 * cols + (head + 1) * HD]
        scores = dot_tn(key, query) * (1.0 / math.sqrt(HD))
        scores = jnp.where(allowed, scores, -1e30)
        scores = jnp.exp(scores - jnp.max(scores, axis=0, keepdims=True))
        weights = (scores / jnp.sum(scores, axis=0, keepdims=True)).astype(BF)
        context[head * HD : (head + 1) * HD, :] = dot_nn(value, weights).astype(BF)
    for shift, out in enumerate((p0, p1, p2, p3)):
        owner = lax.rem(member + shift, 4)
        span = pl.ds(pl.multiple_of(owner * cols, 64), cols)
        out[...] = dot_nn(w_proj[span, :], context[...]).astype(BF)


def attention(member, pieces, gain, w_qkv, b_qkv, w_proj, key_tag, step_rows=256):
    cols, rows = pieces[0].shape
    width = cols * 4
    piece_spec = pl.BlockSpec((cols, step_rows), lambda i, *_: (0, i))
    return pl.pallas_call(
        attention_kernel,
        grid_spec=pltpu.PrefetchScalarGridSpec(
            num_scalar_prefetch=1,
            grid=(rows // step_rows,),
            in_specs=[piece_spec] * 4
            + [
                whole((width, 1)),
                whole((3 * cols, width)),
                whole((3 * cols, 1)),
                whole((width, cols)),
                pl.BlockSpec((step_rows, 1), lambda i, *_: (i, 0)),
            ],
            out_specs=[piece_spec] * 4,
            scratch_shapes=[
                pltpu.VMEM((width, step_rows), BF),
                pltpu.VMEM((cols, step_rows), BF),
            ],
        ),
        out_shape=[jax.ShapeDtypeStruct((cols, rows), BF)] * 4,
        compiler_params=params(),
        cost_estimate=pl.CostEstimate(
            flops=2 * rows * width * cols * 4, bytes_accessed=7 * 2**20, transcendentals=rows * 1024
        ),
        name="attention",
    )(member, *pieces, gain, w_qkv, b_qkv, w_proj, key_tag)


def expand_kernel(member_ref, e0, e1, e2, e3, gain, weight, bias, out, normed, total):
    width, rows = normed.shape
    cols = width // 4
    part = pl.program_id(0)
    member = member_ref[0]

    @pl.when(part == 0)
    def _():
        pieces = [ref[...].astype(F32) for ref in (e0, e1, e2, e3)]
        square = sum(jnp.sum(piece * piece, axis=0, keepdims=True) for piece in pieces)
        inverse = lax.rsqrt(square * (1.0 / width) + EPSILON)
        for shift, piece in enumerate(pieces):
            owner = lax.rem(member - shift + 4, 4)
            span = pl.ds(pl.multiple_of(owner * cols, 64), cols)
            normed[span, :] = (piece * inverse * gain[span, :]).astype(BF)
        total[...] = jnp.zeros_like(total)

    picks_shape = (rows // 4, rows)
    picks = (
        lax.broadcasted_iota(jnp.int32, picks_shape, 1)
        == 4 * lax.broadcasted_iota(jnp.int32, picks_shape, 0) + part
    )
    turned = dot_nt(picks.astype(F32).astype(BF), normed[...]).astype(BF)
    total[...] += dot_nn(turned, weight[...])

    @pl.when(part == 3)
    def _():
        value = total[...] + bias[...]
        out[...] = (0.5 * value * (1.0 + lax.erf(value * (1.0 / math.sqrt(2.0))))).astype(BF)


def expand(member, pieces, gain, weight, bias):
    cols, rows = pieces[0].shape
    width = cols * 4
    hidden = weight.shape[1]
    return pl.pallas_call(
        expand_kernel,
        grid_spec=pltpu.PrefetchScalarGridSpec(
            num_scalar_prefetch=1,
            grid=(4,),
            in_specs=[whole((cols, rows))] * 4
            + [
                whole((width, 1)),
                pl.BlockSpec((width, hidden), lambda i, *_: (i, 0)),
                whole((1, hidden)),
            ],
            out_specs=whole((rows // 4, hidden)),
            scratch_shapes=[
                pltpu.VMEM((width, rows), BF),
                pltpu.VMEM((rows // 4, hidden), F32),
            ],
        ),
        out_shape=jax.ShapeDtypeStruct((rows // 4, hidden), BF),
        compiler_params=params(),
        cost_estimate=pl.CostEstimate(
            flops=2 * rows * width * (hidden + rows // 4),
            bytes_accessed=9 * 2**20,
            transcendentals=rows // 4 * hidden,
        ),
        name="expand",
    )(member, *pieces, gain, weight, bias)


def route_kernel(*refs):
    source, blocks, outs, held = refs[0], refs[1:9], refs[9:17], refs[17]
    rows = blocks[0].shape[0]
    for at, block in enumerate(blocks):
        held[at * rows : (at + 1) * rows, :] = block[...]
    for at, out in enumerate(outs):
        wanted = source[at * rows : (at + 1) * rows, :]
        picks = lax.broadcasted_iota(jnp.int32, (rows, held.shape[0]), 1) == wanted
        out[...] = dot_nn(picks.astype(F32).astype(BF), held[...]).astype(BF)


def route(source, blocks):
    rows, hidden = blocks[0].shape
    return pl.pallas_call(
        route_kernel,
        out_shape=[jax.ShapeDtypeStruct((rows, hidden), BF)] * 8,
        scratch_shapes=[pltpu.VMEM((8 * rows, hidden), BF)],
        compiler_params=params(),
        cost_estimate=pl.CostEstimate(
            flops=2 * 64 * rows * rows * hidden, bytes_accessed=4 * 2**20, transcendentals=0
        ),
        name="route",
    )(source, *blocks)


def output_kernel(member_ref, *refs):
    blocks, weight, outs, held = refs[:8], refs[8], refs[9:13], refs[13]
    part = pl.program_id(0)

    @pl.when(part == 0)
    def _():
        held[...] = sum(block[...].astype(F32) for block in blocks).astype(BF)

    result = dot_nt(held[...], weight[...]).astype(BF)
    for at, out in enumerate(outs):

        @pl.when(part == at)
        def _(out=out):
            out[...] = result


def output_map(member, blocks, weight):
    rows, hidden = blocks[0].shape
    cols = weight.shape[0] // 4
    return pl.pallas_call(
        output_kernel,
        grid_spec=pltpu.PrefetchScalarGridSpec(
            num_scalar_prefetch=1,
            grid=(4,),
            in_specs=[whole((rows, hidden))] * 8
            + [pl.BlockSpec((cols, hidden), lambda i, member: (lax.rem(member[0] + i, 4), 0))],
            out_specs=[whole((rows, cols))] * 4,
            scratch_shapes=[pltpu.VMEM((rows, hidden), BF)],
        ),
        out_shape=[jax.ShapeDtypeStruct((rows, cols), BF)] * 4,
        compiler_params=params(),
        cost_estimate=pl.CostEstimate(
            flops=8 * rows * hidden * cols, bytes_accessed=8 * 2**20, transcendentals=0
        ),
        name="output_map",
    )(member, *blocks, weight)


def place_kernel(p0, p1, p2, p3, bias, source, out):
    total = sum(ref[...].astype(F32) for ref in (p0, p1, p2, p3)) + bias[...]
    rows = p0.shape[0]
    picks = lax.broadcasted_iota(jnp.int32, (out.shape[0], rows), 1) == source[...]
    out[...] = dot_nn(picks.astype(F32).astype(BF), total.astype(BF)).astype(BF)


def place(parts, bias, source):
    cols = parts[0].shape[1]
    return pl.pallas_call(
        place_kernel,
        out_shape=jax.ShapeDtypeStruct((source.shape[0], cols), BF),
        compiler_params=params(),
        name="place",
    )(*parts, bias, source)


def pack_kernel(slot_image, rows_ref, out, packed):
    half = rows_ref.shape[0] // 2
    for image in range(rows_ref.shape[1] // CAP):
        low = rows_ref[:half, image * CAP : (image + 1) * CAP]
        high = rows_ref[half:, image * CAP : (image + 1) * CAP]
        packed[image] = jnp.concatenate([low, high], axis=1)

    @pl.loop(0, out.shape[0])
    def _(slot):
        out[slot] = packed[slot_image[slot]]


def pack(slot_image, rows_t):
    half, images = rows_t.shape[0] // 2, rows_t.shape[1] // CAP
    slots = slot_image.shape[0]
    return pl.pallas_call(
        pack_kernel,
        in_specs=[pl.BlockSpec(memory_space=pltpu.SMEM), pl.BlockSpec(memory_space=pltpu.VMEM)],
        out_shape=jax.ShapeDtypeStruct((slots, half, 2 * CAP), BF),
        scratch_shapes=[pltpu.VMEM((images, half, 2 * CAP), BF)],
        compiler_params=params(),
        name="pack",
    )(slot_image, rows_t)


def unpack_kernel(slot_from, first, second, out):
    half = first.shape[1]
    out[:half, :] = jnp.concatenate([first[0, :, :CAP], second[0, :, :CAP]], axis=1)
    out[half:, :] = jnp.concatenate([first[0, :, CAP:], second[0, :, CAP:]], axis=1)


def unpack(slot_from, landed):
    half = landed.shape[1]
    images = slot_from.shape[0]
    return pl.pallas_call(
        unpack_kernel,
        grid_spec=pltpu.PrefetchScalarGridSpec(
            num_scalar_prefetch=1,
            grid=(images // 2,),
            in_specs=[
                pl.BlockSpec((1, half, 2 * CAP), lambda i, at: (at[2 * i], 0, 0)),
                pl.BlockSpec((1, half, 2 * CAP), lambda i, at: (at[2 * i + 1], 0, 0)),
            ],
            out_specs=pl.BlockSpec((2 * half, 2 * CAP), lambda i, at: (0, i)),
        ),
        out_shape=jax.ShapeDtypeStruct((2 * half, images * CAP), BF),
        compiler_params=params(),
        name="unpack",
    )(slot_from, landed, landed)


def tensor_shift(values, shift):
    return lax.ppermute(values, "tensor", [(i, (i + shift) % 4) for i in range(4)])


def rank_of(y, z, c):
    return ((y % NY) * NZ + z % NZ) * NC + c % NC


def dp_shift(values, dy, dz, dc):
    pairs = [
        (rank_of(y, z, c), rank_of(y + dy, z + dz, c + dc))
        for y in range(NY)
        for z in range(NZ)
        for c in range(NC)
    ]
    return lax.ppermute(values, "dp", pairs)


def per_device(
    patches,
    counts,
    source_slot,
    target_slot,
    lang_start,
    window_order,
    norm_gain,
    qkv_weight,
    qkv_bias,
    proj_weight,
    proj_bias,
    merge_gain,
    expand_weight,
    expand_bias,
    output_weight,
    output_bias,
):
    dp_index = lax.axis_index("dp")
    member = lax.axis_index("tensor")
    rows, cols = patches.shape
    images = rows // CAP
    depth = CAP // 4
    width = cols * 4
    at_y, at_z, at_c = dp_index // (NZ * NC), dp_index // NC % NZ, dp_index % NC
    member_arg = member.reshape(1).astype(jnp.int32)

    own = patches.T
    pieces = [own] + [tensor_shift(own, shift) for shift in (1, 2, 3)]
    expand_full = lax.all_gather(expand_weight, "dp", axis=0, tiled=True)
    output_full = lax.all_gather(output_weight.T, "dp", axis=0, tiled=True)

    slot_ids = dp_index * images + jnp.arange(images, dtype=jnp.int32)
    held = source_slot[None, :] == slot_ids[:, None]
    live_count = jnp.sum(jnp.where(held, counts[None, :], 0), axis=1)
    outward = jnp.sum(jnp.where(held, target_slot[None, :], 0), axis=1) // images
    bound = target_slot[None, :] == slot_ids[:, None]
    slot_from = jnp.sum(jnp.where(bound, source_slot[None, :], 0), axis=1) // images
    rank_ids = jnp.arange(NY * NZ * NC, dtype=jnp.int32)
    slot_image = jnp.sum(
        jnp.where(
            outward[None, :] == rank_ids[:, None], jnp.arange(images, dtype=jnp.int32)[None, :], 0
        ),
        axis=1,
    )
    row_ids = jnp.arange(CAP, dtype=jnp.int32)
    live = row_ids[None, :] < live_count[:, None]
    image_ids = jnp.arange(images, dtype=jnp.int32)
    key_tag = jnp.where(live, image_ids[:, None], -1).reshape(rows, 1)
    live_row = live.reshape(1, rows)

    def plane(table):
        tail = table.shape[1:]
        table = table.reshape(NY, NZ, NC, images, *tail)
        table = lax.dynamic_index_in_dim(table, at_z, 1, keepdims=False)
        table = lax.dynamic_slice_in_dim(jnp.concatenate([table, table], 0), at_y, NY, 0)
        return lax.dynamic_slice_in_dim(jnp.concatenate([table, table], 1), at_c, NC, 1)

    plane_source = plane(source_slot)
    plane_rank = plane_source // images
    here = jnp.logical_and(plane_rank // (NZ * NC) == at_y, plane_rank % NC == at_c)
    step = (at_z - plane_rank // NC % NZ + NZ) % NZ
    base = (step * images + plane_source % images) * depth
    route_source = jnp.where(here[..., None], base[..., None] + plane(window_order), -1)
    route_source = route_source.reshape(NY * NC * images * depth, 1)

    own_start = (
        lax.dynamic_slice_in_dim(lang_start, dp_index * images, images, 0) - dp_index * LROWS
    )
    own_used = lax.dynamic_slice_in_dim(counts, dp_index * images, images, 0) // 4
    lang_rows = jnp.arange(LROWS, dtype=jnp.int32)[:, None]
    inside = jnp.logical_and(
        lang_rows >= own_start[None, :], lang_rows < own_start[None, :] + own_used[None, :]
    )
    place_source = (
        jnp.sum(
            jnp.where(inside, image_ids[None, :] * depth + lang_rows - own_start[None, :] + 1, 0),
            axis=1,
            keepdims=True,
        )
        - 1
    )

    parts = attention(
        member_arg,
        pieces,
        norm_gain.reshape(width, 1),
        qkv_weight.transpose(1, 2, 0).reshape(3 * cols, width),
        qkv_bias.reshape(3 * cols, 1),
        proj_weight.T,
        key_tag,
    )
    arrived = [tensor_shift(parts[shift], shift) for shift in (1, 2, 3)]
    summed = sum(part.astype(F32) for part in [parts[0]] + arrived)
    own_bias = lax.dynamic_slice_in_dim(proj_bias, member * cols, cols, 0)
    hidden = own.astype(F32) + summed + own_bias[:, None]
    encoded_here = jnp.where(live_row, hidden, 0.0).astype(BF)

    encoded_pieces = [encoded_here] + [tensor_shift(encoded_here, shift) for shift in (1, 2, 3)]
    leaving = pack(slot_image, encoded_here)
    landed = lax.all_to_all(leaving, "dp", split_axis=0, concat_axis=0, tiled=True)

    expanded = expand(
        member_arg,
        encoded_pieces,
        merge_gain.reshape(width, 1),
        expand_full,
        expand_bias.reshape(1, -1),
    )
    ring = [expanded] + [dp_shift(expanded, 0, shift, 0) for shift in range(1, NZ)]
    routed = route(route_source, ring)
    blocks = [routed[0]]
    for at in range(1, NY * NC):
        blocks.append(dp_shift(routed[at], at // NC, 0, at % NC))
    out_parts = output_map(member_arg, blocks, output_full)
    out_arrived = [tensor_shift(out_parts[shift], shift) for shift in (1, 2, 3)]
    merged = place([out_parts[0]] + out_arrived, output_bias.reshape(1, -1), place_source)
    encoded = unpack(slot_from, landed).T
    return (encoded, merged)


def solution(mesh):
    in_specs = (
        P("dp", "tensor"),
        P(),
        P(),
        P(),
        P(),
        P(),
        P(),
        P(None, None, "tensor"),
        P(None, "tensor"),
        P("tensor", None),
        P(),
        P(),
        P("dp", "tensor"),
        P("tensor"),
        P("tensor", "dp"),
        P("tensor"),
    )
    out_specs = (P("dp", "tensor"), P("dp", "tensor"))
    return jax.shard_map(
        per_device, mesh=mesh, in_specs=in_specs, out_specs=out_specs, check_vma=False
    )
```

```python
import functools
import math

import jax
import jax.numpy as jnp
from jax import lax
from jax.experimental import pallas as pl
from jax.experimental.pallas import tpu as pltpu
from jax.sharding import Mesh, PartitionSpec as P

HD = 80
CAP = 64
LROWS = 160
NY, NZ, NC = 4, 8, 2
EPSILON = 1e-06
BF = jnp.bfloat16
F32 = jnp.float32


def dot_tn(lhs, rhs):
    return lax.dot_general(lhs, rhs, (((0,), (0,)), ((), ())), preferred_element_type=F32)


def dot_nt(lhs, rhs):
    return lax.dot_general(lhs, rhs, (((1,), (1,)), ((), ())), preferred_element_type=F32)


def dot_nn(lhs, rhs):
    return jnp.dot(lhs, rhs, preferred_element_type=F32)


def params(mib=60):
    return pltpu.CompilerParams(vmem_limit_bytes=mib * 1024 * 1024)


def cost(microseconds):
    return pl.CostEstimate(
        flops=int(microseconds * 3.3e9), bytes_accessed=2**20, transcendentals=0
    )


def whole(shape):
    return pl.BlockSpec(shape, lambda *_: (0,) * len(shape))


def attention_kernel(
    member_ref, a0, a1, a2, a3, gain, w_qkv, b_qkv, w_proj, key_tag, p0, p1, p2, p3, normed, context
):
    width, rows = normed.shape
    cols = width // 4
    heads = cols // HD
    member = member_ref[0]
    pieces = [ref[...].astype(F32) for ref in (a0, a1, a2, a3)]
    square = sum(jnp.sum(piece * piece, axis=0, keepdims=True) for piece in pieces)
    inverse = lax.rsqrt(square * (1.0 / width) + EPSILON)
    for shift, piece in enumerate(pieces):
        owner = lax.rem(member - shift + 4, 4)
        span = pl.ds(pl.multiple_of(owner * cols, 64), cols)
        normed[span, :] = (piece * inverse * gain[span, :]).astype(BF)
    qkv = (dot_nn(w_qkv[...], normed[...]) + b_qkv[...]).astype(BF)
    query_image = lax.broadcasted_iota(jnp.int32, (rows, rows), 1) // CAP + pl.program_id(0) * (
        rows // CAP
    )
    allowed = key_tag[...] == query_image
    for head in range(heads):
        query = qkv[head * HD : (head + 1) * HD]
        key = qkv[cols + head * HD : cols + (head + 1) * HD]
        value = qkv[2 * cols + head * HD : 2 * cols + (head + 1) * HD]
        scores = dot_tn(key, query) * (1.0 / math.sqrt(HD))
        scores = jnp.where(allowed, scores, -1e30)
        scores = jnp.exp(scores - jnp.max(scores, axis=0, keepdims=True))
        weights = (scores / jnp.sum(scores, axis=0, keepdims=True)).astype(BF)
        context[head * HD : (head + 1) * HD, :] = dot_nn(value, weights).astype(BF)
    for shift, out in enumerate((p0, p1, p2, p3)):
        owner = lax.rem(member + shift, 4)
        span = pl.ds(pl.multiple_of(owner * cols, 64), cols)
        out[...] = dot_nn(w_proj[span, :], context[...]).astype(BF)


def attention(member, pieces, gain, w_qkv, b_qkv, w_proj, key_tag, step_rows=256):
    cols, rows = pieces[0].shape
    width = cols * 4
    piece_spec = pl.BlockSpec((cols, step_rows), lambda i, *_: (0, i))
    return pl.pallas_call(
        attention_kernel,
        grid_spec=pltpu.PrefetchScalarGridSpec(
            num_scalar_prefetch=1,
            grid=(rows // step_rows,),
            in_specs=[piece_spec] * 4
            + [
                whole((width, 1)),
                whole((3 * cols, width)),
                whole((3 * cols, 1)),
                whole((width, cols)),
                pl.BlockSpec((step_rows, 1), lambda i, *_: (i, 0)),
            ],
            out_specs=[piece_spec] * 4,
            scratch_shapes=[
                pltpu.VMEM((width, step_rows), BF),
                pltpu.VMEM((cols, step_rows), BF),
            ],
        ),
        out_shape=[jax.ShapeDtypeStruct((cols, rows), BF)] * 4,
        compiler_params=params(20),
        cost_estimate=cost(9),
        name="attention",
    )(member, *pieces, gain, w_qkv, b_qkv, w_proj, key_tag)


def expand_kernel(at_ref, e0, e1, e2, e3, gain, weight, bias, *refs):
    out, normed, turned, total = refs[-4:]
    width, rows = normed.shape
    cols = width // 4
    merged = rows // 4
    shift_y = pl.program_id(0)
    member = at_ref[0]

    @pl.when(shift_y == 0)
    def _():
        pieces = [ref[...].astype(F32) for ref in (e0, e1, e2, e3)]
        square = sum(jnp.sum(piece * piece, axis=0, keepdims=True) for piece in pieces)
        inverse = lax.rsqrt(square * (1.0 / width) + EPSILON)
        for shift, piece in enumerate(pieces):
            owner = lax.rem(member - shift + 4, 4)
            span = pl.ds(pl.multiple_of(owner * cols, 64), cols)
            normed[span, :] = (piece * inverse * gain[span, :]).astype(BF)
        into = lax.broadcasted_iota(jnp.int32, (rows, rows), 0)
        picks = lax.broadcasted_iota(jnp.int32, (rows, rows), 1) == 4 * (
            into % merged
        ) + into // merged
        turned[...] = dot_nt(picks.astype(F32).astype(BF), normed[...]).astype(BF)
        total[...] = jnp.zeros_like(total)

    position = lax.rem(at_ref[1] - shift_y + NY, NY)
    span = pl.ds(pl.multiple_of(position * merged, 128), merged)
    total[...] += dot_nn(turned[span, :], weight[...].reshape(width, total.shape[1]))

    @pl.when(shift_y == NY - 1)
    def _():
        value = total[...] + bias[...]
        out[...] = (0.5 * value * (1.0 + lax.erf(value * (1.0 / math.sqrt(2.0))))).astype(BF)


def expand(at, pieces, gain, weight, bias, after):
    cols, rows = pieces[0].shape
    width = cols * 4
    chunk, hidden = width // (NZ * NC), weight.shape[4]
    return pl.pallas_call(
        expand_kernel,
        grid_spec=pltpu.PrefetchScalarGridSpec(
            num_scalar_prefetch=1,
            grid=(NY,),
            in_specs=[whole((cols, rows))] * 4
            + [
                whole((width, 1)),
                pl.BlockSpec((NZ, NC, 1, chunk, hidden), lambda i, *_: (0, 0, i, 0, 0)),
                whole((1, hidden)),
            ]
            + [pl.BlockSpec(memory_space=pl.ANY)] * len(after),
            out_specs=whole((rows // 4, hidden)),
            scratch_shapes=[
                pltpu.VMEM((width, rows), BF),
                pltpu.VMEM((rows, width), BF),
                pltpu.VMEM((rows // 4, hidden), F32),
            ],
        ),
        out_shape=jax.ShapeDtypeStruct((rows // 4, hidden), BF),
        compiler_params=params(),
        cost_estimate=cost(6),
        name="expand",
    )(at, *pieces, gain, weight, bias, *after)


def route_kernel(*refs):
    source, blocks, outs, held = refs[0], refs[1:9], refs[-9:-1], refs[-1]
    rows = blocks[0].shape[0]
    for at, block in enumerate(blocks):
        held[at * rows : (at + 1) * rows, :] = block[...]
    for at, out in enumerate(outs):
        wanted = source[at * rows : (at + 1) * rows, :]
        picks = lax.broadcasted_iota(jnp.int32, (rows, held.shape[0]), 1) == wanted
        out[...] = dot_nn(picks.astype(F32).astype(BF), held[...]).astype(BF)


def route(source, blocks):
    rows, hidden = blocks[0].shape
    return pl.pallas_call(
        route_kernel,
        out_shape=[jax.ShapeDtypeStruct((rows, hidden), BF)] * 8,
        scratch_shapes=[pltpu.VMEM((8 * rows, hidden), BF)],
        compiler_params=params(),
        cost_estimate=cost(4),
        name="route",
    )(source, *blocks)


def output_kernel(at_ref, *refs):
    blocks, weight, outs, held = refs[:8], refs[8], refs[9:13], refs[13]
    part = pl.program_id(0)

    @pl.when(part == 0)
    def _():
        held[...] = sum(block[...].astype(F32) for block in blocks).astype(BF)

    flat = weight[...].reshape(outs[0].shape[1], held.shape[1])
    result = dot_nt(held[...], flat).astype(BF)
    for at, out in enumerate(outs):

        @pl.when(part == at)
        def _(out=out):
            out[...] = result


def output_map(at, blocks, weight, chunk):
    rows, hidden = blocks[0].shape
    cols = NZ * NC * chunk
    weight = weight.reshape(NZ * NC, weight.shape[1] // chunk, chunk, hidden)
    return pl.pallas_call(
        output_kernel,
        grid_spec=pltpu.PrefetchScalarGridSpec(
            num_scalar_prefetch=1,
            grid=(4,),
            in_specs=[whole((rows, hidden))] * 8
            + [
                pl.BlockSpec(
                    (NZ * NC, 1, chunk, hidden),
                    lambda i, at: (0, lax.rem(at[1] - at[0] - i + 8, 4), 0, 0),
                )
            ],
            out_specs=[whole((rows, cols))] * 4,
            scratch_shapes=[pltpu.VMEM((rows, hidden), BF)],
        ),
        out_shape=[jax.ShapeDtypeStruct((rows, cols), BF)] * 4,
        compiler_params=params(),
        cost_estimate=cost(6),
        name="output_map",
    )(at, *blocks, weight)


def place_kernel(p0, p1, p2, p3, bias, source, out):
    total = sum(ref[...].astype(F32) for ref in (p0, p1, p2, p3)) + bias[...]
    rows = p0.shape[0]
    picks = lax.broadcasted_iota(jnp.int32, (out.shape[0], rows), 1) == source[...]
    out[...] = dot_nn(picks.astype(F32).astype(BF), total.astype(BF)).astype(BF)


def place(parts, bias, source):
    cols = parts[0].shape[1]
    return pl.pallas_call(
        place_kernel,
        out_shape=jax.ShapeDtypeStruct((source.shape[0], cols), BF),
        compiler_params=params(),
        cost_estimate=cost(3),
        name="place",
    )(*parts, bias, source)


def bundle_kernel(rows_ref, *refs):
    out = refs[-1]
    shards = refs[:NY]
    chunk, width = shards[0].shape
    for at, shard in enumerate(shards):
        out[at * chunk : (at + 1) * chunk, :] = shard[...]
    blocks = width // CAP
    depth = rows_ref.shape[0] // blocks
    for image in range(rows_ref.shape[1] // CAP):
        parts = [
            rows_ref[at * depth : (at + 1) * depth, image * CAP : (image + 1) * CAP]
            for at in range(blocks)
        ]
        first = NY * chunk + image * depth
        out[first : first + depth, :] = jnp.concatenate(parts, axis=1)


def bundle(rows_t, shards):
    chunk, width = shards[0].shape
    rows = NY * chunk + rows_t.size // width
    return pl.pallas_call(
        bundle_kernel,
        out_shape=jax.ShapeDtypeStruct((rows, width), BF),
        compiler_params=params(),
        cost_estimate=cost(3),
        name="bundle",
    )(rows_t, *shards)


def spread_kernel(source, bundles, *refs):
    outs, sems = refs[-NY - 1 : -1], refs[-1]
    images, depth, _ = outs[0].shape
    first = bundles.shape[1] - images * depth

    def copy(out, group, slot):
        at = jnp.maximum(source[group * images + slot], 0)
        row = pl.multiple_of(first + at % images * depth, depth)
        return pltpu.make_async_copy(
            bundles.at[at // images, pl.ds(row, depth), :],
            out.at[slot],
            sems.at[group * images + slot],
        )

    for group, out in enumerate(outs):
        out[...] = jnp.zeros_like(out)

        @pl.loop(0, images)
        def _(slot, group=group, out=out):
            @pl.when(source[group * images + slot] >= 0)
            def _():
                copy(out, group, slot).start()

    for group, out in enumerate(outs):

        @pl.loop(0, images)
        def _(slot, group=group, out=out):
            @pl.when(source[group * images + slot] >= 0)
            def _():
                copy(out, group, slot).wait()


def spread(source, bundles, depth, after):
    slots = source.shape[0]
    anywhere = pl.BlockSpec(memory_space=pl.ANY)
    return pl.pallas_call(
        spread_kernel,
        in_specs=[pl.BlockSpec(memory_space=pltpu.SMEM), anywhere] + [anywhere] * len(after),
        out_shape=[jax.ShapeDtypeStruct((slots // NY, depth, bundles.shape[2]), BF)] * NY,
        scratch_shapes=[pltpu.SemaphoreType.DMA((slots,))],
        compiler_params=params(),
        cost_estimate=cost(4),
        name="spread",
    )(source, bundles, *after)


def unpack_kernel(*refs):
    groups, out = refs[:-1], refs[-1]
    count, depth, width = groups[0].shape
    for at in range(count // 2):
        first, second = (
            sum(group[image].astype(F32) for group in groups).astype(BF)
            for image in (2 * at, 2 * at + 1)
        )
        for block in range(width // CAP):
            span = slice(block * CAP, (block + 1) * CAP)
            out[block * depth : (block + 1) * depth, 2 * CAP * at : 2 * CAP * (at + 1)] = (
                jnp.concatenate([first[:, span], second[:, span]], axis=1)
            )


def unpack(groups):
    count, depth, width = groups[0].shape
    return pl.pallas_call(
        unpack_kernel,
        out_shape=jax.ShapeDtypeStruct((depth * width // CAP, count * CAP), BF),
        compiler_params=params(),
        cost_estimate=cost(2),
        name="unpack",
    )(*groups)


def axis_shift(values, axis, size, shift):
    return lax.ppermute(values, axis, [(i, (i + shift) % size) for i in range(size)])


def tensor_shift(values, shift):
    return axis_shift(values, "tensor", 4, shift)


def z_shift(values, shift):
    return axis_shift(values, "z", NZ, shift)


def yc_shift(values, dy, dc):
    pairs = [
        (y * NC + c, (y + dy) % NY * NC + (c + dc) % NC) for y in range(NY) for c in range(NC)
    ]
    return lax.ppermute(values, ("y", "c"), pairs)


def stack_kernel(*refs):
    for at in range(NY):
        refs[-1][at] = refs[at][...]


def stack(values):
    return pl.pallas_call(
        stack_kernel,
        out_shape=jax.ShapeDtypeStruct((NY, *values[0].shape), BF),
        compiler_params=params(),
        cost_estimate=cost(1),
        name="stack",
    )(*values)


def hold_kernel(value, _, out):
    out[...] = value[...]


def hold(value, after):
    in_vmem = pl.BlockSpec(memory_space=pltpu.VMEM)
    return pl.pallas_call(
        hold_kernel,
        in_specs=[in_vmem, pl.BlockSpec(memory_space=pl.ANY)],
        out_shape=jax.ShapeDtypeStruct(value.shape, value.dtype),
        compiler_params=params(),
        cost_estimate=cost(1),
        name="hold",
    )(value, after)


def ring_near(values):
    return {shift: z_shift(values, shift) for shift in (1, -1, 2, -2)}


def ring_far(near):
    return {3: z_shift(near[2], 1), -3: z_shift(near[-2], -1), 4: z_shift(near[2], 2)}


def along_y(shard):
    return [shard] + [axis_shift(shard, "y", NY, shift) for shift in (1, 2, 3)]


def gather_zc(values):
    return lax.all_gather(values, ("z", "c"), axis=0)


def per_device(
    patches,
    counts,
    source_slot,
    target_slot,
    lang_start,
    window_order,
    norm_gain,
    qkv_weight,
    qkv_bias,
    proj_weight,
    proj_bias,
    merge_gain,
    expand_weight,
    expand_bias,
    output_weight,
    output_bias,
):
    at_y, at_z, at_c = lax.axis_index("y"), lax.axis_index("z"), lax.axis_index("c")
    dp_index = (at_y * NZ + at_z) * NC + at_c
    member = lax.axis_index("tensor")
    rows, cols = patches.shape
    images = rows // CAP
    depth = CAP // 4
    width = cols * 4
    at = jnp.stack([member, at_y]).astype(jnp.int32)

    own = patches.T
    pieces = [own] + [tensor_shift(own, shift) for shift in (1, 2, 3)]
    expand_full = gather_zc(stack(along_y(expand_weight)))
    expand_full = expand_full.reshape(NZ, NC, *expand_full.shape[1:])

    slot_ids = dp_index * images + jnp.arange(images, dtype=jnp.int32)
    held = source_slot[None, :] == slot_ids[:, None]
    live_count = jnp.sum(jnp.where(held, counts[None, :], 0), axis=1)
    row_ids = jnp.arange(CAP, dtype=jnp.int32)
    live = row_ids[None, :] < live_count[:, None]
    image_ids = jnp.arange(images, dtype=jnp.int32)
    key_tag = jnp.where(live, image_ids[:, None], -1).reshape(rows, 1)
    live_row = live.reshape(1, rows)

    def plane(table):
        tail = table.shape[1:]
        table = table.reshape(NY, NZ, NC, images, *tail)
        table = lax.dynamic_index_in_dim(table, at_z, 1, keepdims=False)
        table = lax.dynamic_slice_in_dim(jnp.concatenate([table, table], 0), at_y, NY, 0)
        return lax.dynamic_slice_in_dim(jnp.concatenate([table, table], 1), at_c, NC, 1)

    near_slots = ((at_y + jnp.arange(NY)[:, None]) % NY * NZ + at_z) * NC + at_c
    near_slots = (near_slots * images + image_ids).reshape(-1, 1).astype(jnp.int32)
    bound = target_slot[None, :] == near_slots
    bound_source = jnp.sum(jnp.where(bound, source_slot[None, :], 0), axis=1)
    column = NZ * NC * images
    spread_source = jnp.where(bound_source // column == at_y, bound_source % column, -1)

    plane_source = plane(source_slot)
    plane_rank = plane_source // images
    here = jnp.logical_and(plane_rank // (NZ * NC) == at_y, plane_rank % NC == at_c)
    step = (at_z - plane_rank // NC % NZ + NZ) % NZ
    base = (step * images + plane_source % images) * depth
    route_source = jnp.where(here[..., None], base[..., None] + plane(window_order), -1)
    route_source = route_source.reshape(NY * NC * images * depth, 1)

    own_start = (
        lax.dynamic_slice_in_dim(lang_start, dp_index * images, images, 0) - dp_index * LROWS
    )
    own_used = lax.dynamic_slice_in_dim(counts, dp_index * images, images, 0) // 4
    lang_rows = jnp.arange(LROWS, dtype=jnp.int32)[:, None]
    inside = jnp.logical_and(
        lang_rows >= own_start[None, :], lang_rows < own_start[None, :] + own_used[None, :]
    )
    place_source = (
        jnp.sum(
            jnp.where(inside, image_ids[None, :] * depth + lang_rows - own_start[None, :] + 1, 0),
            axis=1,
            keepdims=True,
        )
        - 1
    )

    parts = attention(
        at,
        pieces,
        norm_gain.reshape(width, 1),
        qkv_weight.transpose(1, 2, 0).reshape(3 * cols, width),
        qkv_bias.reshape(3 * cols, 1),
        proj_weight.T,
        key_tag,
    )
    arrived = [tensor_shift(parts[shift], shift) for shift in (1, 2, 3)]
    summed = sum(part.astype(F32) for part in [parts[0]] + arrived)
    own_bias = lax.dynamic_slice_in_dim(proj_bias, member * cols, cols, 0)
    hidden = own.astype(F32) + summed + own_bias[:, None]
    encoded_here = jnp.where(live_row, hidden, 0.0).astype(BF)

    encoded_pieces = [encoded_here] + [tensor_shift(encoded_here, shift) for shift in (1, 2, 3)]
    output_shards = along_y(hold(output_weight.T, parts[0]))
    bundles = gather_zc(bundle(encoded_here, output_shards))
    expanded = expand(
        at,
        encoded_pieces,
        merge_gain.reshape(width, 1),
        expand_full,
        expand_bias.reshape(1, -1),
        [],
    )
    near = ring_near(expanded)
    ring = {0: expanded, **near, **ring_far(near)}
    ring = [ring[shift] if shift in ring else ring[shift - NZ] for shift in range(NZ)]
    routed = route(route_source, ring)
    blocks = [routed[0]]
    for slot in range(1, NY * NC):
        blocks.append(yc_shift(routed[slot], slot // NC, slot % NC))
    packed_depth = rows * cols // images // output_weight.shape[0]
    leaving = spread(spread_source, bundles, packed_depth, blocks[1:])
    landed = [leaving[0]] + [axis_shift(leaving[k], "y", NY, k) for k in (1, 2, 3)]
    out_parts = output_map(at, blocks, bundles, output_weight.shape[1])
    out_arrived = [tensor_shift(out_parts[shift], shift) for shift in (1, 2, 3)]
    merged = place([out_parts[0]] + out_arrived, output_bias.reshape(1, -1), place_source)
    encoded = unpack(landed).T
    return (encoded, merged)


def solution(mesh):
    fine_mesh = Mesh(mesh.devices.reshape(NY, NZ, NC, 4), ("y", "z", "c", "tensor"))
    dp = ("y", "z", "c")
    in_specs = (
        P(dp, "tensor"),
        P(),
        P(),
        P(),
        P(),
        P(),
        P(),
        P(None, None, "tensor"),
        P(None, "tensor"),
        P("tensor", None),
        P(),
        P(),
        P(dp, "tensor"),
        P("tensor"),
        P("tensor", dp),
        P("tensor"),
    )
    out_specs = (P(dp, "tensor"), P(dp, "tensor"))
    return jax.shard_map(
        per_device, mesh=fine_mesh, in_specs=in_specs, out_specs=out_specs, check_vma=False
    )
```

```python
import functools
import math

import jax
import jax.numpy as jnp
from jax import lax
from jax.experimental import pallas as pl
from jax.experimental.pallas import tpu as pltpu
from jax.sharding import Mesh, PartitionSpec as P

HD = 80
CAP = 64
LROWS = 160
NY, NZ, NC = 4, 8, 2
EPSILON = 1e-06
BF = jnp.bfloat16
F32 = jnp.float32


def dot_tn(lhs, rhs):
    return lax.dot_general(lhs, rhs, (((0,), (0,)), ((), ())), preferred_element_type=F32)


def dot_nt(lhs, rhs):
    return lax.dot_general(lhs, rhs, (((1,), (1,)), ((), ())), preferred_element_type=F32)


def dot_nn(lhs, rhs):
    return jnp.dot(lhs, rhs, preferred_element_type=F32)


def params(mib=60):
    return pltpu.CompilerParams(vmem_limit_bytes=mib * 1024 * 1024)


def cost(microseconds):
    return pl.CostEstimate(
        flops=int(microseconds * 3.3e9), bytes_accessed=2**20, transcendentals=0
    )


def whole(shape):
    return pl.BlockSpec(shape, lambda *_: (0,) * len(shape))


def attention_kernel(
    member_ref, a0, a1, a2, a3, gain, w_qkv, b_qkv, w_proj, key_tag, p0, p1, p2, p3, normed, context
):
    width, rows = normed.shape
    cols = width // 4
    heads = cols // HD
    member = member_ref[0]
    pieces = [ref[...].astype(F32) for ref in (a0, a1, a2, a3)]
    square = sum(jnp.sum(piece * piece, axis=0, keepdims=True) for piece in pieces)
    inverse = lax.rsqrt(square * (1.0 / width) + EPSILON)
    for shift, piece in enumerate(pieces):
        owner = lax.rem(member - shift + 4, 4)
        span = pl.ds(pl.multiple_of(owner * cols, 64), cols)
        normed[span, :] = (piece * inverse * gain[span, :1]).astype(BF)
    qkv = (dot_nn(w_qkv[...], normed[...]) + b_qkv[...]).astype(BF)
    query_image = lax.broadcasted_iota(jnp.int32, (rows, rows), 1) // CAP + pl.program_id(0) * (
        rows // CAP
    )
    allowed = key_tag[...] == query_image
    for head in range(heads):
        query = qkv[head * HD : (head + 1) * HD]
        key = qkv[cols + head * HD : cols + (head + 1) * HD]
        value = qkv[2 * cols + head * HD : 2 * cols + (head + 1) * HD]
        scores = dot_tn(key, query) * (1.0 / math.sqrt(HD))
        scores = jnp.where(allowed, scores, -1e30)
        scores = jnp.exp(scores - jnp.max(scores, axis=0, keepdims=True))
        weights = (scores / jnp.sum(scores, axis=0, keepdims=True)).astype(BF)
        context[head * HD : (head + 1) * HD, :] = dot_nn(value, weights).astype(BF)
    for shift, out in enumerate((p0, p1, p2, p3)):
        owner = lax.rem(member + shift, 4)
        span = pl.ds(pl.multiple_of(owner * cols, 64), cols)
        out[...] = dot_nn(w_proj[span, :], context[...]).astype(BF)


def attention(member, pieces, gain, w_qkv, b_qkv, w_proj, key_tag, step_rows=256):
    cols, rows = pieces[0].shape
    width = cols * 4
    piece_spec = pl.BlockSpec((cols, step_rows), lambda i, *_: (0, i))
    return pl.pallas_call(
        attention_kernel,
        grid_spec=pltpu.PrefetchScalarGridSpec(
            num_scalar_prefetch=1,
            grid=(rows // step_rows,),
            in_specs=[piece_spec] * 4
            + [
                whole((width, 2)),
                whole((3 * cols, width)),
                whole((3 * cols, 1)),
                whole((width, cols)),
                pl.BlockSpec((step_rows, 1), lambda i, *_: (i, 0)),
            ],
            out_specs=[piece_spec] * 4,
            scratch_shapes=[
                pltpu.VMEM((width, step_rows), BF),
                pltpu.VMEM((cols, step_rows), BF),
            ],
        ),
        out_shape=[jax.ShapeDtypeStruct((cols, rows), BF)] * 4,
        compiler_params=params(20),
        cost_estimate=cost(9),
        name="attention",
    )(member, *pieces, gain, w_qkv, b_qkv, w_proj, key_tag)


def expand_kernel(at_ref, e0, e1, e2, e3, gain, weight, bias, *refs):
    out, normed, turned, total = refs[-4:]
    width, rows = normed.shape
    cols = width // 4
    merged = rows // 4
    shift_y = pl.program_id(0)
    member = at_ref[0]

    @pl.when(shift_y == 0)
    def _():
        pieces = [ref[...].astype(F32) for ref in (e0, e1, e2, e3)]
        square = sum(jnp.sum(piece * piece, axis=0, keepdims=True) for piece in pieces)
        inverse = lax.rsqrt(square * (1.0 / width) + EPSILON)
        for shift, piece in enumerate(pieces):
            owner = lax.rem(member - shift + 4, 4)
            span = pl.ds(pl.multiple_of(owner * cols, 64), cols)
            normed[span, :] = (piece * inverse * gain[span, 1:]).astype(BF)
        into = lax.broadcasted_iota(jnp.int32, (rows, rows), 0)
        picks = lax.broadcasted_iota(jnp.int32, (rows, rows), 1) == 4 * (
            into % merged
        ) + into // merged
        turned[...] = dot_nt(picks.astype(F32).astype(BF), normed[...]).astype(BF)
        total[...] = jnp.zeros_like(total)

    position = lax.rem(at_ref[1] - shift_y + NY, NY)
    span = pl.ds(pl.multiple_of(position * merged, 128), merged)
    total[...] += dot_nn(turned[span, :], weight[...].reshape(width, total.shape[1]))

    @pl.when(shift_y == NY - 1)
    def _():
        value = total[...] + bias[...]
        out[...] = (0.5 * value * (1.0 + lax.erf(value * (1.0 / math.sqrt(2.0))))).astype(BF)


def expand(at, pieces, gain, weight, bias, after):
    cols, rows = pieces[0].shape
    width = cols * 4
    chunk, hidden = width // (NZ * NC), weight.shape[4]
    return pl.pallas_call(
        expand_kernel,
        grid_spec=pltpu.PrefetchScalarGridSpec(
            num_scalar_prefetch=1,
            grid=(NY,),
            in_specs=[whole((cols, rows))] * 4
            + [
                whole((width, 2)),
                pl.BlockSpec((NZ, NC, 1, chunk, hidden), lambda i, *_: (0, 0, i, 0, 0)),
                whole((1, hidden)),
            ]
            + [pl.BlockSpec(memory_space=pl.ANY)] * len(after),
            out_specs=whole((rows // 4, hidden)),
            scratch_shapes=[
                pltpu.VMEM((width, rows), BF),
                pltpu.VMEM((rows, width), BF),
                pltpu.VMEM((rows // 4, hidden), F32),
            ],
        ),
        out_shape=jax.ShapeDtypeStruct((rows // 4, hidden), BF),
        compiler_params=params(),
        cost_estimate=cost(6),
        name="expand",
    )(at, *pieces, gain, weight, bias, *after)


def route_kernel(*refs):
    source, blocks, (same, other), held = refs[0], refs[1:9], refs[9:11], refs[11]
    rows = blocks[0].shape[0]
    for at, block in enumerate(blocks):
        held[at * rows : (at + 1) * rows, :] = block[...]
    for at in range(NY * NC):
        wanted = source[at * rows : (at + 1) * rows, :]
        picks = lax.broadcasted_iota(jnp.int32, (rows, held.shape[0]), 1) == wanted
        out = (same, other)[at % NC]
        out[at // NC] = dot_nn(picks.astype(F32).astype(BF), held[...]).astype(BF)


def route(source, blocks):
    rows, hidden = blocks[0].shape
    return pl.pallas_call(
        route_kernel,
        out_shape=[jax.ShapeDtypeStruct((NY, rows, hidden), BF)] * NC,
        scratch_shapes=[pltpu.VMEM((8 * rows, hidden), BF)],
        compiler_params=params(),
        cost_estimate=cost(4),
        name="route",
    )(source, *blocks)


def merge_kernel(same, other, *outs):
    for at, out in enumerate(outs):
        out[...] = (same[at].astype(F32) + other[at].astype(F32)).astype(BF)


def merge(same, other):
    return pl.pallas_call(
        merge_kernel,
        out_shape=[jax.ShapeDtypeStruct(same.shape[1:], BF)] * NY,
        compiler_params=params(),
        cost_estimate=cost(1),
        name="merge",
    )(same, other)


def output_kernel(at_ref, *refs):
    blocks, weight, outs, held = refs[:NY], refs[NY], refs[-5:-1], refs[-1]
    part = pl.program_id(0)

    @pl.when(part == 0)
    def _():
        held[...] = sum(block[...].astype(F32) for block in blocks).astype(BF)

    flat = weight[...].reshape(outs[0].shape[1], held.shape[1])
    result = dot_nt(held[...], flat).astype(BF)
    for at, out in enumerate(outs):

        @pl.when(part == at)
        def _(out=out):
            out[...] = result


def output_map(at, blocks, weight, chunk):
    rows, hidden = blocks[0].shape
    cols = NZ * NC * chunk
    weight = weight.reshape(NZ * NC, weight.shape[1] // chunk, chunk, hidden)
    return pl.pallas_call(
        output_kernel,
        grid_spec=pltpu.PrefetchScalarGridSpec(
            num_scalar_prefetch=1,
            grid=(4,),
            in_specs=[whole((rows, hidden))] * NY
            + [
                pl.BlockSpec(
                    (NZ * NC, 1, chunk, hidden),
                    lambda i, at: (0, lax.rem(at[1] - at[0] - i + 8, 4), 0, 0),
                )
            ],
            out_specs=[whole((rows, cols))] * 4,
            scratch_shapes=[pltpu.VMEM((rows, hidden), BF)],
        ),
        out_shape=[jax.ShapeDtypeStruct((rows, cols), BF)] * 4,
        compiler_params=params(),
        cost_estimate=cost(6),
        name="output_map",
    )(at, *blocks, weight)


def place_kernel(p0, p1, p2, p3, bias, source, out):
    total = sum(ref[...].astype(F32) for ref in (p0, p1, p2, p3)) + bias[...]
    rows = p0.shape[0]
    picks = lax.broadcasted_iota(jnp.int32, (out.shape[0], rows), 1) == source[...]
    out[...] = dot_nn(picks.astype(F32).astype(BF), total.astype(BF)).astype(BF)


def place(parts, bias, source):
    cols = parts[0].shape[1]
    return pl.pallas_call(
        place_kernel,
        out_shape=jax.ShapeDtypeStruct((source.shape[0], cols), BF),
        compiler_params=params(),
        cost_estimate=cost(3),
        name="place",
    )(*parts, bias, source)


def bundle_kernel(rows_ref, *refs):
    out = refs[-1]
    shards = refs[:NY]
    chunk, width = shards[0].shape
    for at, shard in enumerate(shards):
        out[at * chunk : (at + 1) * chunk, :] = shard[...]
    blocks = width // CAP
    depth = rows_ref.shape[0] // blocks
    for image in range(rows_ref.shape[1] // CAP):
        parts = [
            rows_ref[at * depth : (at + 1) * depth, image * CAP : (image + 1) * CAP]
            for at in range(blocks)
        ]
        first = NY * chunk + image * depth
        out[first : first + depth, :] = jnp.concatenate(parts, axis=1)


def bundle(rows_t, shards):
    chunk, width = shards[0].shape
    rows = NY * chunk + rows_t.size // width
    return pl.pallas_call(
        bundle_kernel,
        out_shape=jax.ShapeDtypeStruct((rows, width), BF),
        compiler_params=params(),
        cost_estimate=cost(3),
        name="bundle",
    )(rows_t, *shards)


def spread_kernel(source, bundles, *refs):
    outs, sems = refs[-NY - 1 : -1], refs[-1]
    images, depth, _ = outs[0].shape
    first = bundles.shape[1] - images * depth

    def copy(out, group, slot):
        at = jnp.maximum(source[group * images + slot], 0)
        row = pl.multiple_of(first + at % images * depth, depth)
        return pltpu.make_async_copy(
            bundles.at[at // images, pl.ds(row, depth), :],
            out.at[slot],
            sems.at[group * images + slot],
        )

    for group, out in enumerate(outs):
        out[...] = jnp.zeros_like(out)

        @pl.loop(0, images)
        def _(slot, group=group, out=out):
            @pl.when(source[group * images + slot] >= 0)
            def _():
                copy(out, group, slot).start()

    for group, out in enumerate(outs):

        @pl.loop(0, images)
        def _(slot, group=group, out=out):
            @pl.when(source[group * images + slot] >= 0)
            def _():
                copy(out, group, slot).wait()


def spread(source, bundles, depth, after):
    slots = source.shape[0]
    anywhere = pl.BlockSpec(memory_space=pl.ANY)
    return pl.pallas_call(
        spread_kernel,
        in_specs=[pl.BlockSpec(memory_space=pltpu.SMEM), anywhere] + [anywhere] * len(after),
        out_shape=[jax.ShapeDtypeStruct((slots // NY, depth, bundles.shape[2]), BF)] * NY,
        scratch_shapes=[pltpu.SemaphoreType.DMA((slots,))],
        compiler_params=params(),
        cost_estimate=cost(4),
        name="spread",
    )(source, bundles, *after)


def unpack_kernel(*refs):
    groups, out = refs[:-1], refs[-1]
    count, depth, width = groups[0].shape
    for at in range(count // 2):
        first, second = (
            sum(group[image].astype(F32) for group in groups).astype(BF)
            for image in (2 * at, 2 * at + 1)
        )
        for block in range(width // CAP):
            span = slice(block * CAP, (block + 1) * CAP)
            out[block * depth : (block + 1) * depth, 2 * CAP * at : 2 * CAP * (at + 1)] = (
                jnp.concatenate([first[:, span], second[:, span]], axis=1)
            )


def unpack(groups):
    count, depth, width = groups[0].shape
    return pl.pallas_call(
        unpack_kernel,
        out_shape=jax.ShapeDtypeStruct((depth * width // CAP, count * CAP), BF),
        compiler_params=params(),
        cost_estimate=cost(2),
        name="unpack",
    )(*groups)


def axis_shift(values, axis, size, shift):
    return lax.ppermute(values, axis, [(i, (i + shift) % size) for i in range(size)])


def tensor_shift(values, shift):
    return axis_shift(values, "tensor", 4, shift)


def z_shift(values, shift):
    return axis_shift(values, "z", NZ, shift)


def stack_kernel(*refs):
    for at in range(NY):
        refs[-1][at] = refs[at][...]


def stack(values):
    return pl.pallas_call(
        stack_kernel,
        out_shape=jax.ShapeDtypeStruct((NY, *values[0].shape), BF),
        compiler_params=params(),
        cost_estimate=cost(1),
        name="stack",
    )(*values)


def hold_kernel(value, _, out):
    out[...] = value[...]


def hold(value, after):
    in_vmem = pl.BlockSpec(memory_space=pltpu.VMEM)
    return pl.pallas_call(
        hold_kernel,
        in_specs=[in_vmem, pl.BlockSpec(memory_space=pl.ANY)],
        out_shape=jax.ShapeDtypeStruct(value.shape, value.dtype),
        compiler_params=params(),
        cost_estimate=cost(1),
        name="hold",
    )(value, after)


def ring_near(values):
    return {shift: z_shift(values, shift) for shift in (1, -1, 2, -2)}


def ring_far(near):
    return {3: z_shift(near[2], 1), -3: z_shift(near[-2], -1), 4: z_shift(near[2], 2)}


def along_y(shard):
    return [shard] + [axis_shift(shard, "y", NY, shift) for shift in (1, 2, 3)]


def gather_zc(values):
    return lax.all_gather(values, ("z", "c"), axis=0)


def per_device(
    patches,
    counts,
    source_slot,
    target_slot,
    lang_start,
    window_order,
    norm_gain,
    qkv_weight,
    qkv_bias,
    proj_weight,
    proj_bias,
    merge_gain,
    expand_weight,
    expand_bias,
    output_weight,
    output_bias,
):
    at_y, at_z, at_c = lax.axis_index("y"), lax.axis_index("z"), lax.axis_index("c")
    dp_index = (at_y * NZ + at_z) * NC + at_c
    member = lax.axis_index("tensor")
    rows, cols = patches.shape
    images = rows // CAP
    depth = CAP // 4
    width = cols * 4
    at = jnp.stack([member, at_y]).astype(jnp.int32)

    own = patches.T
    expand_full = gather_zc(stack(along_y(expand_weight)))
    expand_full = expand_full.reshape(NZ, NC, *expand_full.shape[1:])

    slot_ids = dp_index * images + jnp.arange(images, dtype=jnp.int32)
    held = source_slot[None, :] == slot_ids[:, None]
    live_count = jnp.sum(jnp.where(held, counts[None, :], 0), axis=1)
    row_ids = jnp.arange(CAP, dtype=jnp.int32)
    live = row_ids[None, :] < live_count[:, None]
    image_ids = jnp.arange(images, dtype=jnp.int32)
    key_tag = jnp.where(live, image_ids[:, None] % (images // 2), -1).reshape(rows, 1)
    live_row = live.reshape(1, rows)

    def plane(table):
        tail = table.shape[1:]
        table = table.reshape(NY, NZ, NC, images, *tail)
        table = lax.dynamic_index_in_dim(table, at_z, 1, keepdims=False)
        table = lax.dynamic_slice_in_dim(jnp.concatenate([table, table], 0), at_y, NY, 0)
        return lax.dynamic_slice_in_dim(jnp.concatenate([table, table], 1), at_c, NC, 1)

    near_slots = ((at_y + jnp.arange(NY)[:, None]) % NY * NZ + at_z) * NC + at_c
    near_slots = (near_slots * images + image_ids).reshape(-1, 1).astype(jnp.int32)
    bound = target_slot[None, :] == near_slots
    bound_source = jnp.sum(jnp.where(bound, source_slot[None, :], 0), axis=1)
    column = NZ * NC * images
    spread_source = jnp.where(bound_source // column == at_y, bound_source % column, -1)

    plane_source = plane(source_slot)
    plane_rank = plane_source // images
    here = jnp.logical_and(plane_rank // (NZ * NC) == at_y, plane_rank % NC == at_c)
    step = (at_z - plane_rank // NC % NZ + NZ) % NZ
    base = (step * images + plane_source % images) * depth
    route_source = jnp.where(here[..., None], base[..., None] + plane(window_order), -1)
    route_source = route_source.reshape(NY * NC * images * depth, 1)

    own_start = (
        lax.dynamic_slice_in_dim(lang_start, dp_index * images, images, 0) - dp_index * LROWS
    )
    own_used = lax.dynamic_slice_in_dim(counts, dp_index * images, images, 0) // 4
    lang_rows = jnp.arange(LROWS, dtype=jnp.int32)[:, None]
    inside = jnp.logical_and(
        lang_rows >= own_start[None, :], lang_rows < own_start[None, :] + own_used[None, :]
    )
    place_source = (
        jnp.sum(
            jnp.where(inside, image_ids[None, :] * depth + lang_rows - own_start[None, :] + 1, 0),
            axis=1,
            keepdims=True,
        )
        - 1
    )

    gains = jnp.stack([norm_gain, merge_gain], axis=1)
    w_qkv = qkv_weight.transpose(1, 2, 0).reshape(3 * cols, width)
    own_bias = lax.dynamic_slice_in_dim(proj_bias, member * cols, cols, 0)
    w_proj, b_qkv = proj_weight.T, qkv_bias.reshape(3 * cols, 1)
    half = rows // 2
    encoded_halves = []
    for at_half in range(2):
        span = slice(at_half * half, (at_half + 1) * half)
        mine = own[:, span]
        pieces = [mine] + [tensor_shift(mine, shift) for shift in (1, 2, 3)]
        parts = attention(at, pieces, gains, w_qkv, b_qkv, w_proj, key_tag[span])
        arrived = [tensor_shift(parts[shift], shift) for shift in (1, 2, 3)]
        summed = sum(part.astype(F32) for part in [parts[0]] + arrived)
        hidden = mine.astype(F32) + summed + own_bias[:, None]
        encoded_halves.append(jnp.where(live_row[:, span], hidden, 0.0).astype(BF))
    encoded_here = jnp.concatenate(encoded_halves, axis=1)
    encoded_pieces = [encoded_here] + [tensor_shift(encoded_here, shift) for shift in (1, 2, 3)]
    output_shards = along_y(hold(output_weight.T, parts[0]))
    bundles = gather_zc(bundle(encoded_here, output_shards))
    expanded = expand(
        at,
        encoded_pieces,
        gains,
        expand_full,
        expand_bias.reshape(1, -1),
        [],
    )
    near = ring_near(expanded)
    ring = {0: expanded, **near, **ring_far(near)}
    ring = [ring[shift] if shift in ring else ring[shift - NZ] for shift in range(NZ)]
    routed = route(route_source, ring)
    merged_cores = merge(routed[0], axis_shift(routed[1], "c", NC, 1))
    blocks = [merged_cores[0]] + [axis_shift(merged_cores[k], "y", NY, k) for k in (1, 2, 3)]
    packed_depth = rows * cols // images // output_weight.shape[0]
    leaving = spread(spread_source, bundles, packed_depth, blocks[1:2])
    landed = [leaving[0]] + [axis_shift(leaving[k], "y", NY, k) for k in (1, 2, 3)]
    out_parts = output_map(at, blocks, bundles, output_weight.shape[1])
    out_arrived = [tensor_shift(out_parts[shift], shift) for shift in (1, 2, 3)]
    merged = place([out_parts[0]] + out_arrived, output_bias.reshape(1, -1), place_source)
    encoded = unpack(landed).T
    return (encoded, merged)


def solution(mesh):
    fine_mesh = Mesh(mesh.devices.reshape(NY, NZ, NC, 4), ("y", "z", "c", "tensor"))
    dp = ("y", "z", "c")
    in_specs = (
        P(dp, "tensor"),
        P(),
        P(),
        P(),
        P(),
        P(),
        P(),
        P(None, None, "tensor"),
        P(None, "tensor"),
        P("tensor", None),
        P(),
        P(),
        P(dp, "tensor"),
        P("tensor"),
        P("tensor", dp),
        P("tensor"),
    )
    out_specs = (P(dp, "tensor"), P(dp, "tensor"))
    return jax.shard_map(
        per_device, mesh=fine_mesh, in_specs=in_specs, out_specs=out_specs, check_vma=False
    )
```

```python
import functools
import math

import jax
import jax.numpy as jnp
from jax import lax
from jax.experimental import pallas as pl
from jax.experimental.pallas import tpu as pltpu
from jax.sharding import Mesh, PartitionSpec as P

HD = 80
CAP = 64
LROWS = 160
NY, NZ, NC = 4, 8, 2
EPSILON = 1e-06
BF = jnp.bfloat16
F32 = jnp.float32


def dot_tn(lhs, rhs):
    return lax.dot_general(lhs, rhs, (((0,), (0,)), ((), ())), preferred_element_type=F32)


def dot_nt(lhs, rhs):
    return lax.dot_general(lhs, rhs, (((1,), (1,)), ((), ())), preferred_element_type=F32)


def dot_nn(lhs, rhs):
    return jnp.dot(lhs, rhs, preferred_element_type=F32)


def params(mib=60):
    return pltpu.CompilerParams(vmem_limit_bytes=mib * 1024 * 1024)


def cost(microseconds):
    return pl.CostEstimate(
        flops=int(microseconds * 3.3e9), bytes_accessed=2**20, transcendentals=0
    )


def whole(shape):
    return pl.BlockSpec(shape, lambda *_: (0,) * len(shape))


def attention_kernel(
    member_ref, a0, a1, a2, a3, gain, w_qkv, b_qkv, w_proj, key_tag, p0, p1, p2, p3, normed, context
):
    width, rows = normed.shape
    cols = width // 4
    heads = cols // HD
    member = member_ref[0]
    pieces = [ref[...].astype(F32) for ref in (a0, a1, a2, a3)]
    square = sum(jnp.sum(piece * piece, axis=0, keepdims=True) for piece in pieces)
    inverse = lax.rsqrt(square * (1.0 / width) + EPSILON)
    for shift, piece in enumerate(pieces):
        owner = lax.rem(member - shift + 4, 4)
        span = pl.ds(pl.multiple_of(owner * cols, 64), cols)
        normed[span, :] = (piece * inverse * gain[span, :1]).astype(BF)
    qkv = (dot_nn(w_qkv[...], normed[...]) + b_qkv[...]).astype(BF)
    query_image = lax.broadcasted_iota(jnp.int32, (rows, rows), 1) // CAP + pl.program_id(0) * (
        rows // CAP
    )
    allowed = key_tag[...] == query_image
    for head in range(heads):
        query = qkv[head * HD : (head + 1) * HD]
        key = qkv[cols + head * HD : cols + (head + 1) * HD]
        value = qkv[2 * cols + head * HD : 2 * cols + (head + 1) * HD]
        scores = dot_tn(key, query) * (1.0 / math.sqrt(HD))
        scores = jnp.where(allowed, scores, -1e30)
        scores = jnp.exp(scores - jnp.max(scores, axis=0, keepdims=True))
        weights = (scores / jnp.sum(scores, axis=0, keepdims=True)).astype(BF)
        context[head * HD : (head + 1) * HD, :] = dot_nn(value, weights).astype(BF)
    for shift, out in enumerate((p0, p1, p2, p3)):
        owner = lax.rem(member + shift, 4)
        span = pl.ds(pl.multiple_of(owner * cols, 64), cols)
        out[...] = dot_nn(w_proj[span, :], context[...]).astype(BF)


def attention(member, pieces, gain, w_qkv, b_qkv, w_proj, key_tag, step_rows=256):
    cols, rows = pieces[0].shape
    width = cols * 4
    piece_spec = pl.BlockSpec((cols, step_rows), lambda i, *_: (0, i))
    return pl.pallas_call(
        attention_kernel,
        grid_spec=pltpu.PrefetchScalarGridSpec(
            num_scalar_prefetch=1,
            grid=(rows // step_rows,),
            in_specs=[piece_spec] * 4
            + [
                whole((width, 2)),
                whole((3 * cols, width)),
                whole((3 * cols, 1)),
                whole((width, cols)),
                pl.BlockSpec((step_rows, 1), lambda i, *_: (i, 0)),
            ],
            out_specs=[piece_spec] * 4,
            scratch_shapes=[
                pltpu.VMEM((width, step_rows), BF),
                pltpu.VMEM((cols, step_rows), BF),
            ],
        ),
        out_shape=[jax.ShapeDtypeStruct((cols, rows), BF)] * 4,
        compiler_params=params(20),
        cost_estimate=cost(9),
        name="attention",
    )(member, *pieces, gain, w_qkv, b_qkv, w_proj, key_tag)


def expand_kernel(at_ref, e0, e1, e2, e3, gain, weight, bias, *refs):
    out, normed, turned, total = refs[-4:]
    width, rows = normed.shape
    cols = width // 4
    merged = rows // 4
    shift_y = pl.program_id(0)
    member = at_ref[0]

    @pl.when(shift_y == 0)
    def _():
        pieces = [ref[...].astype(F32) for ref in (e0, e1, e2, e3)]
        square = sum(jnp.sum(piece * piece, axis=0, keepdims=True) for piece in pieces)
        inverse = lax.rsqrt(square * (1.0 / width) + EPSILON)
        for shift, piece in enumerate(pieces):
            owner = lax.rem(member - shift + 4, 4)
            span = pl.ds(pl.multiple_of(owner * cols, 64), cols)
            normed[span, :] = (piece * inverse * gain[span, 1:]).astype(BF)
        into = lax.broadcasted_iota(jnp.int32, (rows, rows), 0)
        picks = lax.broadcasted_iota(jnp.int32, (rows, rows), 1) == 4 * (
            into % merged
        ) + into // merged
        turned[...] = dot_nt(picks.astype(F32).astype(BF), normed[...]).astype(BF)
        total[...] = jnp.zeros_like(total)

    position = lax.rem(at_ref[1] - shift_y + NY, NY)
    span = pl.ds(pl.multiple_of(position * merged, 128), merged)
    total[...] += dot_nn(turned[span, :], weight[...].reshape(width, total.shape[1]))

    @pl.when(shift_y == NY - 1)
    def _():
        value = total[...] + bias[...]
        out[...] = (0.5 * value * (1.0 + lax.erf(value * (1.0 / math.sqrt(2.0))))).astype(BF)


def expand(at, pieces, gain, weight, bias, after):
    cols, rows = pieces[0].shape
    width = cols * 4
    chunk, hidden = width // (NZ * NC), weight.shape[4]
    return pl.pallas_call(
        expand_kernel,
        grid_spec=pltpu.PrefetchScalarGridSpec(
            num_scalar_prefetch=1,
            grid=(NY,),
            in_specs=[whole((cols, rows))] * 4
            + [
                whole((width, 2)),
                pl.BlockSpec((NZ, NC, 1, chunk, hidden), lambda i, *_: (0, 0, i, 0, 0)),
                whole((1, hidden)),
            ]
            + [pl.BlockSpec(memory_space=pl.ANY)] * len(after),
            out_specs=whole((rows // 4, hidden)),
            scratch_shapes=[
                pltpu.VMEM((width, rows), BF),
                pltpu.VMEM((rows, width), BF),
                pltpu.VMEM((rows // 4, hidden), F32),
            ],
        ),
        out_shape=jax.ShapeDtypeStruct((rows // 4, hidden), BF),
        compiler_params=params(),
        cost_estimate=cost(6),
        name="expand",
    )(at, *pieces, gain, weight, bias, *after)


def route_kernel(*refs):
    source, blocks, (same, other), held = refs[0], refs[1:9], refs[9:11], refs[11]
    rows = blocks[0].shape[0]
    for at, block in enumerate(blocks):
        held[at * rows : (at + 1) * rows, :] = block[...]
    for at in range(NY * NC):
        wanted = source[at * rows : (at + 1) * rows, :]
        picks = lax.broadcasted_iota(jnp.int32, (rows, held.shape[0]), 1) == wanted
        out = (same, other)[at % NC]
        out[at // NC] = dot_nn(picks.astype(F32).astype(BF), held[...]).astype(BF)


def route(source, blocks):
    rows, hidden = blocks[0].shape
    return pl.pallas_call(
        route_kernel,
        out_shape=[jax.ShapeDtypeStruct((NY, rows, hidden), BF)] * NC,
        scratch_shapes=[pltpu.VMEM((8 * rows, hidden), BF)],
        compiler_params=params(),
        cost_estimate=cost(4),
        name="route",
    )(source, *blocks)


def merge_kernel(same, other, *outs):
    for at, out in enumerate(outs):
        out[...] = (same[at].astype(F32) + other[at].astype(F32)).astype(BF)


def merge(same, other):
    return pl.pallas_call(
        merge_kernel,
        out_shape=[jax.ShapeDtypeStruct(same.shape[1:], BF)] * NY,
        compiler_params=params(),
        cost_estimate=cost(1),
        name="merge",
    )(same, other)


def output_kernel(at_ref, *refs):
    blocks, weight, outs, held = refs[:NY], refs[NY], refs[-5:-1], refs[-1]
    part = pl.program_id(0)

    @pl.when(part == 0)
    def _():
        held[...] = sum(block[...].astype(F32) for block in blocks).astype(BF)

    flat = weight[...].reshape(outs[0].shape[1], held.shape[1])
    result = dot_nt(held[...], flat).astype(BF)
    for at, out in enumerate(outs):

        @pl.when(part == at)
        def _(out=out):
            out[...] = result


def output_map(at, blocks, weight, chunk, after):
    rows, hidden = blocks[0].shape
    cols = NZ * NC * chunk
    weight = weight.reshape(NZ * NC, weight.shape[1] // chunk, chunk, hidden)
    return pl.pallas_call(
        output_kernel,
        grid_spec=pltpu.PrefetchScalarGridSpec(
            num_scalar_prefetch=1,
            grid=(4,),
            in_specs=[whole((rows, hidden))] * NY
            + [
                pl.BlockSpec(
                    (NZ * NC, 1, chunk, hidden),
                    lambda i, at: (0, lax.rem(at[1] - at[0] - i + 8, 4), 0, 0),
                ),
                pl.BlockSpec(memory_space=pl.ANY),
            ],
            out_specs=[whole((rows, cols))] * 4,
            scratch_shapes=[pltpu.VMEM((rows, hidden), BF)],
        ),
        out_shape=[jax.ShapeDtypeStruct((rows, cols), BF)] * 4,
        compiler_params=params(),
        cost_estimate=cost(6),
        name="output_map",
    )(at, *blocks, weight, after)


def place_kernel(p0, p1, p2, p3, bias, source, _, out):
    total = sum(ref[...].astype(F32) for ref in (p0, p1, p2, p3)) + bias[...]
    rows = p0.shape[0]
    picks = lax.broadcasted_iota(jnp.int32, (out.shape[0], rows), 1) == source[...]
    out[...] = dot_nn(picks.astype(F32).astype(BF), total.astype(BF)).astype(BF)


def place(parts, bias, source, after):
    cols = parts[0].shape[1]
    return pl.pallas_call(
        place_kernel,
        out_shape=jax.ShapeDtypeStruct((source.shape[0], cols), BF),
        in_specs=[pl.BlockSpec(memory_space=pltpu.VMEM)] * 6 + [pl.BlockSpec(memory_space=pl.ANY)],
        compiler_params=params(),
        cost_estimate=cost(3),
        name="place",
    )(*parts, bias, source, after)


def bundle_kernel(rows_ref, *refs):
    out = refs[-1]
    shards = refs[:NY]
    chunk, width = shards[0].shape
    for at, shard in enumerate(shards):
        out[at * chunk : (at + 1) * chunk, :] = shard[...]
    blocks = width // CAP
    depth = rows_ref.shape[0] // blocks
    for image in range(rows_ref.shape[1] // CAP):
        parts = [
            rows_ref[at * depth : (at + 1) * depth, image * CAP : (image + 1) * CAP]
            for at in range(blocks)
        ]
        first = NY * chunk + image * depth
        out[first : first + depth, :] = jnp.concatenate(parts, axis=1)


def bundle(rows_t, shards):
    chunk, width = shards[0].shape
    rows = NY * chunk + rows_t.size // width
    return pl.pallas_call(
        bundle_kernel,
        out_shape=jax.ShapeDtypeStruct((rows, width), BF),
        compiler_params=params(),
        cost_estimate=cost(3),
        name="bundle",
    )(rows_t, *shards)


def spread_kernel(source, bundles, *refs):
    outs, sems = refs[-NY - 1 : -1], refs[-1]
    images, depth, _ = outs[0].shape
    first = bundles.shape[1] - images * depth

    def copy(out, group, slot):
        at = jnp.maximum(source[group * images + slot], 0)
        row = pl.multiple_of(first + at % images * depth, depth)
        return pltpu.make_async_copy(
            bundles.at[at // images, pl.ds(row, depth), :],
            out.at[slot],
            sems.at[group * images + slot],
        )

    for group, out in enumerate(outs):
        out[...] = jnp.zeros_like(out)

        @pl.loop(0, images)
        def _(slot, group=group, out=out):
            @pl.when(source[group * images + slot] >= 0)
            def _():
                copy(out, group, slot).start()

    for group, out in enumerate(outs):

        @pl.loop(0, images)
        def _(slot, group=group, out=out):
            @pl.when(source[group * images + slot] >= 0)
            def _():
                copy(out, group, slot).wait()


def spread(source, bundles, depth, after):
    slots = source.shape[0]
    anywhere = pl.BlockSpec(memory_space=pl.ANY)
    return pl.pallas_call(
        spread_kernel,
        in_specs=[pl.BlockSpec(memory_space=pltpu.SMEM), anywhere] + [anywhere] * len(after),
        out_shape=[jax.ShapeDtypeStruct((slots // NY, depth, bundles.shape[2]), BF)] * NY,
        scratch_shapes=[pltpu.SemaphoreType.DMA((slots,))],
        compiler_params=params(),
        cost_estimate=cost(4),
        name="spread",
    )(source, bundles, *after)


def unpack_kernel(*refs):
    groups, out = refs[:-1], refs[-1]
    count, depth, width = groups[0].shape
    for at in range(count // 2):
        first, second = (
            sum(group[image].astype(F32) for group in groups).astype(BF)
            for image in (2 * at, 2 * at + 1)
        )
        for block in range(width // CAP):
            span = slice(block * CAP, (block + 1) * CAP)
            out[block * depth : (block + 1) * depth, 2 * CAP * at : 2 * CAP * (at + 1)] = (
                jnp.concatenate([first[:, span], second[:, span]], axis=1)
            )


def unpack(groups):
    count, depth, width = groups[0].shape
    return pl.pallas_call(
        unpack_kernel,
        out_shape=jax.ShapeDtypeStruct((depth * width // CAP, count * CAP), BF),
        compiler_params=params(),
        cost_estimate=cost(2),
        name="unpack",
    )(*groups)


def axis_shift(values, axis, size, shift):
    return lax.ppermute(values, axis, [(i, (i + shift) % size) for i in range(size)])


def shift_all(values, axis):
    moved = {k: axis_shift(values[k], axis, 4, k) for k in (2, 1, 3)}
    return [values[0]] + [moved[k] for k in (1, 2, 3)]


def z_shift(values, shift):
    return axis_shift(values, "z", NZ, shift)


def stack_kernel(*refs):
    for at in range(NY):
        refs[-1][at] = refs[at][...]


def stack(values):
    return pl.pallas_call(
        stack_kernel,
        out_shape=jax.ShapeDtypeStruct((NY, *values[0].shape), BF),
        compiler_params=params(),
        cost_estimate=cost(1),
        name="stack",
    )(*values)


def hold_kernel(value, _, out):
    out[...] = value[...]


def hold(value, after):
    in_vmem = pl.BlockSpec(memory_space=pltpu.VMEM)
    return pl.pallas_call(
        hold_kernel,
        in_specs=[in_vmem, pl.BlockSpec(memory_space=pl.ANY)],
        out_shape=jax.ShapeDtypeStruct(value.shape, value.dtype),
        compiler_params=params(),
        cost_estimate=cost(1),
        name="hold",
    )(value, after)


def ring_z(values):
    ring = {0: values}
    for step in (1, 2, 3):
        ring[step] = z_shift(ring[step - 1], 1)
        ring[-step] = z_shift(ring[1 - step], -1)
    ring[4] = z_shift(ring[3], 1)
    return [ring[k] if k in ring else ring[k - NZ] for k in range(NZ)]


def stack_kernel(*refs):
    for at in range(NY):
        refs[-1][at] = refs[at][...]


def stack(values):
    return pl.pallas_call(
        stack_kernel,
        out_shape=jax.ShapeDtypeStruct((NY, *values[0].shape), BF),
        compiler_params=params(),
        cost_estimate=cost(1),
        name="stack",
    )(*values)


def hold_kernel(value, _, out):
    out[...] = value[...]


def hold(value, after):
    in_vmem = pl.BlockSpec(memory_space=pltpu.VMEM)
    return pl.pallas_call(
        hold_kernel,
        in_specs=[in_vmem, pl.BlockSpec(memory_space=pl.ANY)],
        out_shape=jax.ShapeDtypeStruct(value.shape, value.dtype),
        compiler_params=params(),
        cost_estimate=cost(1),
        name="hold",
    )(value, after)


def ring_near(values):
    return {shift: z_shift(values, shift) for shift in (1, -1, 2, -2)}


def ring_far(near):
    return {3: z_shift(near[2], 1), -3: z_shift(near[-2], -1), 4: z_shift(near[2], 2)}


def along_y(shard):
    return shift_all([shard] * NY, "y")


def gather_zc(values):
    return lax.all_gather(values, ("z", "c"), axis=0)


def per_device(
    patches,
    counts,
    source_slot,
    target_slot,
    lang_start,
    window_order,
    norm_gain,
    qkv_weight,
    qkv_bias,
    proj_weight,
    proj_bias,
    merge_gain,
    expand_weight,
    expand_bias,
    output_weight,
    output_bias,
):
    at_y, at_z, at_c = lax.axis_index("y"), lax.axis_index("z"), lax.axis_index("c")
    dp_index = (at_y * NZ + at_z) * NC + at_c
    member = lax.axis_index("tensor")
    rows, cols = patches.shape
    images = rows // CAP
    depth = CAP // 4
    width = cols * 4
    at = jnp.stack([member, at_y]).astype(jnp.int32)

    own = patches.T
    expand_full = gather_zc(stack(along_y(expand_weight)))
    expand_full = expand_full.reshape(NZ, NC, *expand_full.shape[1:])

    slot_ids = dp_index * images + jnp.arange(images, dtype=jnp.int32)
    held = source_slot[None, :] == slot_ids[:, None]
    live_count = jnp.sum(jnp.where(held, counts[None, :], 0), axis=1)
    row_ids = jnp.arange(CAP, dtype=jnp.int32)
    live = row_ids[None, :] < live_count[:, None]
    image_ids = jnp.arange(images, dtype=jnp.int32)
    key_tag = jnp.where(live, image_ids[:, None] % (images // 2), -1).reshape(rows, 1)
    live_row = live.reshape(1, rows)

    def plane(table):
        tail = table.shape[1:]
        table = table.reshape(NY, NZ, NC, images, *tail)
        table = lax.dynamic_index_in_dim(table, at_z, 1, keepdims=False)
        table = lax.dynamic_slice_in_dim(jnp.concatenate([table, table], 0), at_y, NY, 0)
        return lax.dynamic_slice_in_dim(jnp.concatenate([table, table], 1), at_c, NC, 1)

    near_slots = ((at_y + jnp.arange(NY)[:, None]) % NY * NZ + at_z) * NC + at_c
    near_slots = (near_slots * images + image_ids).reshape(-1, 1).astype(jnp.int32)
    bound = target_slot[None, :] == near_slots
    bound_source = jnp.sum(jnp.where(bound, source_slot[None, :], 0), axis=1)
    column = NZ * NC * images
    spread_source = jnp.where(bound_source // column == at_y, bound_source % column, -1)

    plane_source = plane(source_slot)
    plane_rank = plane_source // images
    here = jnp.logical_and(plane_rank // (NZ * NC) == at_y, plane_rank % NC == at_c)
    step = (at_z - plane_rank // NC % NZ + NZ) % NZ
    base = (step * images + plane_source % images) * depth
    route_source = jnp.where(here[..., None], base[..., None] + plane(window_order), -1)
    route_source = route_source.reshape(NY * NC * images * depth, 1)

    own_start = (
        lax.dynamic_slice_in_dim(lang_start, dp_index * images, images, 0) - dp_index * LROWS
    )
    own_used = lax.dynamic_slice_in_dim(counts, dp_index * images, images, 0) // 4
    lang_rows = jnp.arange(LROWS, dtype=jnp.int32)[:, None]
    inside = jnp.logical_and(
        lang_rows >= own_start[None, :], lang_rows < own_start[None, :] + own_used[None, :]
    )
    place_source = (
        jnp.sum(
            jnp.where(inside, image_ids[None, :] * depth + lang_rows - own_start[None, :] + 1, 0),
            axis=1,
            keepdims=True,
        )
        - 1
    )

    gains = jnp.stack([norm_gain, merge_gain], axis=1)
    w_qkv = qkv_weight.transpose(1, 2, 0).reshape(3 * cols, width)
    own_bias = lax.dynamic_slice_in_dim(proj_bias, member * cols, cols, 0)
    w_proj, b_qkv = proj_weight.T, qkv_bias.reshape(3 * cols, 1)
    half = rows // 2
    encoded_halves = []
    for at_half in range(2):
        span = slice(at_half * half, (at_half + 1) * half)
        mine = own[:, span]
        pieces = shift_all([mine] * 4, "tensor")
        parts = attention(at, pieces, gains, w_qkv, b_qkv, w_proj, key_tag[span])
        if at_half == 0:
            output_shards = along_y(hold(output_weight.T, parts[0]))
        summed = sum(part.astype(F32) for part in shift_all(parts, "tensor"))
        hidden = mine.astype(F32) + summed + own_bias[:, None]
        encoded_halves.append(jnp.where(live_row[:, span], hidden, 0.0).astype(BF))
    encoded_here = jnp.concatenate(encoded_halves, axis=1)
    encoded_pieces = shift_all([encoded_here] * 4, "tensor")
    bundles = gather_zc(bundle(encoded_here, output_shards))
    expanded = expand(
        at,
        encoded_pieces,
        gains,
        expand_full,
        expand_bias.reshape(1, -1),
        [],
    )
    ring = ring_z(expanded)
    routed = route(route_source, ring)
    merged_cores = merge(routed[0], axis_shift(routed[1], "c", NC, 1))
    blocks = shift_all(merged_cores, "y")
    packed_depth = rows * cols // images // output_weight.shape[0]
    leaving = spread(spread_source, bundles, packed_depth, blocks[1:2])
    landed = shift_all(leaving, "y")
    out_parts = output_map(at, blocks, bundles, output_weight.shape[1], leaving[0])
    encoded_t = unpack(landed)
    merged = place(
        shift_all(out_parts, "tensor"), output_bias.reshape(1, -1), place_source, encoded_t
    )
    encoded = encoded_t.T
    return (encoded, merged)


def solution(mesh):
    fine_mesh = Mesh(mesh.devices.reshape(NY, NZ, NC, 4), ("y", "z", "c", "tensor"))
    dp = ("y", "z", "c")
    in_specs = (
        P(dp, "tensor"),
        P(),
        P(),
        P(),
        P(),
        P(),
        P(),
        P(None, None, "tensor"),
        P(None, "tensor"),
        P("tensor", None),
        P(),
        P(),
        P(dp, "tensor"),
        P("tensor"),
        P("tensor", dp),
        P("tensor"),
    )
    out_specs = (P(dp, "tensor"), P(dp, "tensor"))
    return jax.shard_map(
        per_device, mesh=fine_mesh, in_specs=in_specs, out_specs=out_specs, check_vma=False
    )
```
